32 devices in a mesh: groups: 2 (over y), dev: 8 (over z, x), tp: 1, sub: 2 (over core).
Axes of the slice: x: 2, y: 2, z: 4, core: 2. Of those that a mesh axis runs over, the one named last changes fastest.
Arguments:
- hidden: bfloat16 [256, 4096], P(('groups', 'dev'), ('tp', 'sub')), parts along dimension 0, may hold values from -8 to 8
- new_query: bfloat16 [256, 4096], P(('groups', 'tp', 'sub'), 'dev'), parts along dimension 0, may hold values from -6 to 6
- new_key: bfloat16 [256, 4096], P(('groups', 'tp', 'sub'), 'dev'), parts along dimension 0, may hold values from -6 to 6
- new_value: bfloat16 [256, 4096], P(('groups', 'tp', 'sub'), 'dev'), parts along dimension 0, may hold values from -6 to 6
- out_gate: bfloat16 [256, 4096], P(('groups', 'tp', 'sub'), 'dev'), parts along dimension 0, may hold values from -6 to 6
- states: bfloat16 [256, 32, 128, 128], P(('groups', 'tp', 'sub'), 'dev'), parts along dimension 0, may hold values from -6 to 6
- decay_rate: float32 [32], P('dev'), may hold values from 0.03 to 3
- out_proj: bfloat16 [4096, 4096], P('dev', ('tp', 'sub')), may hold values from -0.09375 to 0.09375
- norm_gain: float32 [4096], P(('tp', 'sub')), may hold values from 0.5 to 2
- routes: int32 [256, 2], P(('groups', 'dev')), parts along dimension 0, may hold values from 0 to 3, all different within a row; in each aligned block of 16 rows (0 to 15, 16 to 31, ...) at most 16 rows name the same one
- route_weight: float32 [256, 2], P(('groups', 'dev')), parts along dimension 0, may hold values from 0.2 to 1
- expert_gate: bfloat16 [8, 4096, 2304], P('dev', ('tp', 'sub')), may hold values from -0.09375 to 0.09375
- expert_up: bfloat16 [8, 4096, 2304], P('dev', ('tp', 'sub')), may hold values from -0.09375 to 0.09375
- expert_down: bfloat16 [8, 2304, 4096], P('dev', None, ('tp', 'sub')), may hold values from -0.09375 to 0.09375
Outputs:
- mixed: bfloat16 [256, 4096], P(('groups', 'dev'), ('tp', 'sub')), parts along dimension 0
- new_states: bfloat16 [256, 32, 128, 128], P(('groups', 'tp', 'sub'), 'dev'), parts along dimension 0
The draws below stay inside these ranges and needn't reach their ends.
There are 2 independent parts, one for each index of `groups`. The reference program is written for one: setup_inputs(seed, part) draws one part's arguments, and reference() takes and returns one part's arrays. A program takes and returns all parts, laid end to end along the dimension named above; an argument that names none is the same for every part. Nothing has to cross between parts.
Inputs may be any that keep to these rules, and one draw needn't show every extreme that they name: `routes`: the 2 experts of a request differ. In the rows of one index of dev (16 requests) no expert is named by more than 16 rows, a bound that some block reaches.
All inputs are finite; a program needn't handle non-finite values.
Results may differ from the reference program's by a relative error of at most 0.012.
Values may be sent and summed in bfloat16 or wider, within the bound.
A program may use at most 128 MiB of HBM per device.

```python
import math
import jax
import jax.numpy as jnp
import numpy as np
from jax import lax

D = 4096
HEADS = 32
HD = 128
FF = 4608
SPLIT = 2
TOP = 2
REQ_DEV = 16
EXPERTS = 4
REQS = 128
CAP = 16


def draw_hidden(key, part):
    key = jax.random.fold_in(key, 11)
    first, second, third = jax.random.split(key, 3)
    ramp = jnp.arange(D, dtype=jnp.float32) / D
    row_scale = jnp.exp(jax.random.uniform(second, (REQS, 1), minval=0.0, maxval=math.log(10.0)))
    noise = jax.random.normal(first, (REQS, D))
    col_scale = jnp.exp(math.log(3.0) * ramp + jax.random.uniform(third, (D,), minval=0.0, maxval=math.log(3.4)))
    values = 0.15 * row_scale * noise * col_scale[None, :]
    return jnp.clip(values, -8.0, 8.0).astype(jnp.bfloat16)


def levels(own_key, shape, shards, least, largest):
    gain, own = 1.0, jax.random.fold_in(own_key, 6)
    for dim, parts in shards:
        heights = jnp.exp(jax.random.uniform(jax.random.fold_in(own, dim), (parts,), jnp.float32, least / len(shards), largest / len(shards)))
        gain = gain * jnp.repeat(heights, shape[dim] // parts).reshape([-1 if axis == dim else 1 for axis in range(len(shape))])
    return gain


def routed_block(rng, own, number, rows, count, top, most, lean):
    order = jax.random.permutation(rng, count)
    crowded, usual = shares(count, rows * top, most, lean, True), shares(count, rows * top, most, lean, False)
    places = jnp.arange(count)

    def named(sizes, turn):
        used = int((sizes > 0).sum())
        fixed = max(1, used // 4)
        shifted = fixed + (places - fixed + turn * (used - fixed)) % max(1, count - fixed)
        return jnp.zeros((count,), jnp.int32).at[order[jnp.where(places < fixed, places, shifted)]].set(jnp.asarray(sizes, jnp.int32))

    sizes = jnp.where(number % 4 == 0, named(crowded, number // 4), named(usual, number - number // 4 - 1))
    mixed = jax.random.permutation(jax.random.fold_in(own, 3), count)
    giver, sink = mixed[0:count // 2 * 2:2], mixed[1:count // 2 * 2:2]
    room = jnp.minimum(sizes[giver] - 1, most - sizes[sink]) // 2
    room = jnp.where((giver == order[0]) | (sink == order[0]) | (sizes[sink] == 0), 0, jnp.maximum(room, 0))
    shifted = jax.random.randint(jax.random.fold_in(own, 4), (count // 2,), 0, 1 << 20) % (room + 1)
    sizes = sizes.at[giver].add(-shifted).at[sink].add(shifted)
    items = jnp.searchsorted(jnp.cumsum(sizes), jnp.arange(rows * top), side="right").astype(jnp.int32)
    listing = items.reshape(top, rows).T
    listing = listing[jax.random.permutation(jax.random.fold_in(own, 1), rows)]
    turn = jax.random.randint(jax.random.fold_in(own, 2), (rows, 1), 0, top)
    return jnp.take_along_axis(listing, (jnp.arange(top)[None, :] + turn) % top, axis=1)


def shares(number_of, total, reach, slope, full):
    weights = [(1 << 20) // math.isqrt(grade ** slope) + 1 for grade in range(1, number_of + 1)]
    largest = reach if full else min(reach, max(-(-total // number_of), total * weights[0] // sum(weights)))
    least = 1 if total - largest >= number_of - 1 else 0
    counts, spare = [largest] + [least] * (number_of - 1), total - largest - least * (number_of - 1)
    while spare > 0:
        candidates = [i for i in range(1, number_of) if counts[i] < largest] or [i for i in range(1, number_of) if counts[i] < reach]
        mass, left = sum([weights[i] for i in candidates]), spare
        for i in candidates:
            addition = min(reach - counts[i], max(1, left * weights[i] // mass), spare)
            counts[i] = counts[i] + addition
            spare = spare - addition
    return np.array(counts)


def gaussian(key, dims, deviation, reach, pieces=(), held_as=jnp.bfloat16):
    loudness = levels(key, dims, pieces, -0.22, 0.18) if pieces else 1.0
    values = jax.random.normal(key, dims, jnp.float32) * deviation * loudness
    return jnp.minimum(jnp.maximum(values, -reach), reach).astype(held_as)


def setup_inputs(seed: int = 0, part: int = 0) -> dict:
    key_of = jax.random.split(jax.random.key(seed), 15)
    part_keys = jax.random.split(jax.random.fold_in(key_of[14], part), 15)
    hidden = draw_hidden(jax.random.fold_in(jax.random.fold_in(key_of[14], part), 71), part)
    new_query = gaussian(part_keys[1], (REQS, HEADS * HD), 1.0, 6.0, ((0, 2), (1, 8)))
    new_key = gaussian(part_keys[2], (REQS, HEADS * HD), 1.0, 6.0, ((0, 2), (1, 8)))
    new_value = gaussian(part_keys[3], (REQS, HEADS * HD), 1.0, 6.0, ((0, 2), (1, 8)))
    out_gate = gaussian(part_keys[4], (REQS, HEADS * HD), 1.5, 6.0, ((0, 2), (1, 8)))
    states = gaussian(part_keys[5], (REQS, HEADS, HD, HD), 1.0, 6.0, ((0, 2), (1, 8)))
    decay_rate = jnp.clip(jnp.exp(math.log(3.0) - 4.6051702 * jax.random.uniform(key_of[6], (HEADS,), jnp.float32) ** levels(key_of[6], (HEADS,), ((0, 8),), -0.2, 0.2)), 0.03, 3.0)
    out_proj = gaussian(key_of[7], (HEADS * HD, D), (HEADS * HD) ** -0.5, 0.09375, ((0, 8), (1, 2)))
    norm_gain = jnp.clip(jnp.exp(math.log(2.0) - 1.3862944 * jax.random.uniform(key_of[8], (D,), jnp.float32) ** levels(key_of[8], (D,), ((0, 2),), -0.2, 0.2)), 0.5, 2.0)
    routes_keys = jax.random.split(jax.random.fold_in(part_keys[9], 1), REQS // REQ_DEV)
    routes_turns = jax.random.permutation(jax.random.fold_in(part_keys[9], 3), REQS // REQ_DEV)
    routes = jax.vmap(lambda own, number: routed_block(jax.random.fold_in(part_keys[9], 2), own, number, REQ_DEV, EXPERTS, TOP, CAP, 2))(routes_keys, routes_turns).reshape((REQS, TOP))
    route_weight = jnp.clip(0.2 + 0.8 * jax.random.uniform(part_keys[10], (REQS, TOP), jnp.float32) ** levels(part_keys[10], (REQS, TOP), ((0, 8),), -0.2, 0.2), 0.2, 1.0)
    expert_gate = gaussian(key_of[11], (EXPERTS * SPLIT, D, FF // SPLIT), D ** -0.5, 0.09375, ((0, 8), (1, 2)))
    expert_up = gaussian(key_of[12], (EXPERTS * SPLIT, D, FF // SPLIT), D ** -0.5, 0.09375, ((0, 8), (1, 2)))
    expert_down = gaussian(key_of[13], (EXPERTS * SPLIT, FF // SPLIT, D), FF ** -0.5, 0.09375, ((0, 8), (2, 2)))
    return {"hidden": hidden, "new_query": new_query, "new_key": new_key, "new_value": new_value, "out_gate": out_gate, "states": states, "decay_rate": decay_rate, "out_proj": out_proj, "norm_gain": norm_gain, "routes": routes, "route_weight": route_weight, "expert_gate": expert_gate, "expert_up": expert_up, "expert_down": expert_down}


EPS = 1e-06

def reference(hidden, new_query, new_key, new_value, out_gate, states, decay_rate, out_proj, norm_gain, routes, route_weight, expert_gate, expert_up, expert_down):
    count = hidden.shape[0]
    query_heads = new_query.astype(jnp.float32).reshape(count, HEADS, HD) * HD ** (-0.5)
    key_heads = new_key.astype(jnp.float32).reshape(count, HEADS, HD)
    value_heads = new_value.astype(jnp.float32).reshape(count, HEADS, HD)
    retain = jnp.exp(-decay_rate)
    updated = retain[None, :, None, None] * states.astype(jnp.float32) + key_heads[:, :, :, None] * value_heads[:, :, None, :]
    readout = jnp.einsum('rhi,rhij->rhj', query_heads, updated, precision=lax.Precision.HIGHEST)
    head_out = (jax.nn.sigmoid(out_gate.astype(jnp.float32)) * readout.reshape(count, HEADS * HD)).astype(jnp.bfloat16)
    attended = jnp.dot(head_out, out_proj, preferred_element_type=jnp.float32)
    residual = (hidden.astype(jnp.float32) + attended).astype(jnp.bfloat16)
    resid_f = residual.astype(jnp.float32)
    inverse = lax.rsqrt(lax.optimization_barrier(jnp.mean(resid_f * resid_f, axis=1)) + EPS)[:, None]
    scaled = (resid_f * norm_gain[None, :]).astype(jnp.bfloat16)
    part_width = FF // SPLIT
    gate_all = expert_gate.reshape(EXPERTS, SPLIT, D, part_width).transpose(0, 2, 1, 3).reshape(EXPERTS, D, FF)
    up_all = expert_up.reshape(EXPERTS, SPLIT, D, part_width).transpose(0, 2, 1, 3).reshape(EXPERTS, D, FF)
    down_all = expert_down.reshape(EXPERTS, FF, D)

    def one_expert(weights):
        gate_w, up_w, down_w = weights
        gate = inverse * jnp.dot(scaled, gate_w, preferred_element_type=jnp.float32)
        upward = inverse * jnp.dot(scaled, up_w, preferred_element_type=jnp.float32)
        act = (jax.nn.silu(gate) * upward).astype(jnp.bfloat16)
        return jnp.dot(act, down_w, preferred_element_type=jnp.float32)
    outputs = lax.map(one_expert, (gate_all, up_all, down_all))
    chosen = routes[:, :, None] == jnp.arange(EXPERTS, dtype=jnp.int32)[None, None, :]
    coeff = lax.optimization_barrier(jnp.sum(jnp.where(chosen, route_weight[:, :, None], jnp.float32(0.0)), axis=1))
    mixture = jnp.einsum('ne,end->nd', coeff, outputs, precision=lax.Precision.HIGHEST)
    mixed = (resid_f + mixture).astype(jnp.bfloat16)
    return (mixed, updated.astype(jnp.bfloat16))
```

```python
import jax
import jax.numpy as jnp
from jax import lax
from jax.experimental import pallas as pl
from jax.experimental.pallas import tpu as pltpu
from jax.sharding import PartitionSpec as P

D = 4096
SPLIT = 2


EPS = 1e-06


def route_tables(routes, route_weight, experts, slots):
    expert_ids = jnp.arange(experts, dtype=jnp.int32)
    chosen = routes[:, :, None] == expert_ids[None, None, :]
    member = jnp.any(chosen, axis=1).astype(jnp.int32)
    position = jnp.cumsum(member, axis=0) - member
    slot_ids = jnp.arange(slots, dtype=jnp.int32)
    placed = (member[:, :, None] == 1) & (position[:, :, None] == slot_ids[None, None, :])
    weights = jnp.sum(jnp.where(chosen, route_weight[:, :, None], jnp.float32(0.0)), axis=1)
    return (placed, weights)


def shards(
    hidden,
    new_query,
    new_key,
    new_value,
    out_gate,
    states,
    decay_rate,
    out_proj,
    norm_gain,
    routes,
    route_weight,
    expert_gate,
    expert_up,
    expert_down,
):
    local_reqs = states.shape[0]
    heads_here = states.shape[1]
    head_size = states.shape[3]
    query_heads = new_query.astype(jnp.float32).reshape(
        local_reqs, heads_here, head_size
    ) * head_size ** (-0.5)
    key_heads = new_key.astype(jnp.float32).reshape(local_reqs, heads_here, head_size)
    value_heads = new_value.astype(jnp.float32).reshape(local_reqs, heads_here, head_size)
    retain = jnp.exp(-decay_rate)
    updated = (
        retain[None, :, None, None] * states.astype(jnp.float32)
        + key_heads[:, :, :, None] * value_heads[:, :, None, :]
    )
    readout = jnp.einsum("rhi,rhij->rhj", query_heads, updated, precision=lax.Precision.HIGHEST)
    head_out = (
        jax.nn.sigmoid(out_gate.astype(jnp.float32))
        * readout.reshape(local_reqs, heads_here * head_size)
    ).astype(jnp.bfloat16)
    new_states = updated.astype(jnp.bfloat16)
    all_heads = lax.all_gather(head_out, ("tp", "sub"), axis=0, tiled=True)
    rows_here = hidden.shape[0]
    attended = lax.psum_scatter(
        jnp.dot(all_heads, out_proj, preferred_element_type=jnp.float32),
        "dev",
        scatter_dimension=0,
        tiled=True,
    )
    residual = (hidden.astype(jnp.float32) + attended).astype(jnp.bfloat16)
    feature_count = residual.shape[1]
    experts = lax.axis_size("dev") // SPLIT
    top_count = routes.shape[1]
    slots = min(rows_here, 2 * ((rows_here * top_count + experts - 1) // experts))
    placed, weights = route_tables(routes, route_weight, experts, slots)
    picks = placed.astype(jnp.bfloat16)
    outgoing = jnp.einsum(
        "nec,nd->ecd", picks, residual, preferred_element_type=jnp.float32
    ).astype(jnp.bfloat16)
    outgoing = jnp.repeat(outgoing, SPLIT, axis=0)
    received = lax.all_to_all(outgoing, "dev", split_axis=0, concat_axis=0, tiled=True)
    sources, count, width = received.shape
    flat_rows = received.reshape(sources * count, width).astype(jnp.float32)
    scaled = (flat_rows * norm_gain[None, :]).astype(jnp.bfloat16)
    gate_part = jnp.dot(scaled, expert_gate[0], preferred_element_type=jnp.float32)
    up_part = jnp.dot(scaled, expert_up[0], preferred_element_type=jnp.float32)
    squares = jnp.sum(flat_rows * flat_rows, axis=1)
    gate_sum, up_sum, square_sum = lax.psum((gate_part, up_part, squares), ("tp", "sub"))
    inverse = lax.rsqrt(square_sum / D + EPS)[:, None]
    act = (jax.nn.silu(inverse * gate_sum) * (inverse * up_sum)).astype(jnp.bfloat16)
    produced = jnp.dot(act, expert_down[0], preferred_element_type=jnp.float32)
    expert_out = produced.reshape(sources, count, width)
    returned = lax.all_to_all(expert_out, "dev", split_axis=0, concat_axis=0, tiled=True)
    merged = returned.reshape(experts, SPLIT, slots, feature_count).sum(axis=1)
    coeff = placed.astype(jnp.float32) * weights[:, :, None]
    mixture = jnp.einsum("nec,ecd->nd", coeff, merged, precision=lax.Precision.HIGHEST)
    mixed = (residual.astype(jnp.float32) + mixture).astype(jnp.bfloat16)
    return (mixed, new_states)


ROWS = 16
HEAD_STEP = 2
PIECES = 4
TILE = 256
MESH = pl.DeviceIdType.MESH


def state_kernel(q_ref, k_ref, v_ref, g_ref, s_ref, d_ref, new_ref, out_ref):
    rows, heads, size = s_ref.shape[0], s_ref.shape[1], s_ref.shape[3]
    row_ids = lax.broadcasted_iota(jnp.int32, (rows, size), 0)
    for h in range(heads):
        lanes = pl.ds(h * size, size)
        q = q_ref[:, lanes]
        q32 = q.astype(jnp.float32)
        k32 = k_ref[:, lanes].astype(jnp.float32)
        v32 = v_ref[:, lanes].astype(jnp.float32)
        columns = k32.T
        retain = jnp.exp(-d_ref[h])
        read = jnp.zeros((rows, size), jnp.float32)
        for r in range(rows):
            state = s_ref[r, h]
            product = jnp.dot(q, state, preferred_element_type=jnp.float32)
            read = jnp.where(row_ids == r, product, read)
            new_ref[r, h] = (
                retain * state.astype(jnp.float32) + columns[:, r : r + 1] * v32[r : r + 1, :]
            ).astype(jnp.bfloat16)
        overlap = jnp.sum(q32 * k32, axis=1, keepdims=True)
        read = (retain * read + overlap * v32) * size ** (-0.5)
        gate = g_ref[:, lanes].astype(jnp.float32)
        out_ref[:, lanes] = (read / (1.0 + jnp.exp(-gate))).astype(jnp.bfloat16)


def update_states(new_query, new_key, new_value, out_gate, states, decay_rate):
    reqs, heads, size = states.shape[0], states.shape[1], states.shape[3]
    flat = pl.BlockSpec((ROWS, HEAD_STEP * size), lambda i, j: (i, j))
    block = pl.BlockSpec((ROWS, HEAD_STEP, size, size), lambda i, j: (i, j, 0, 0))
    return pl.pallas_call(
        state_kernel,
        grid=(reqs // ROWS, heads // HEAD_STEP),
        in_specs=[flat, flat, flat, flat, block, pl.BlockSpec((HEAD_STEP, 1, 1), lambda i, j: (j, 0, 0))],
        out_specs=[block, flat],
        out_shape=[
            jax.ShapeDtypeStruct(states.shape, jnp.bfloat16),
            jax.ShapeDtypeStruct((reqs, heads * size), jnp.bfloat16),
        ],
        compiler_params=pltpu.CompilerParams(vmem_limit_bytes=40 * 2**20),
        name="states",
    )(new_query, new_key, new_value, out_gate, states, decay_rate.reshape(heads, 1, 1))


def send(src, dst, send_sem, recv_sem, **target):
    return pltpu.make_async_remote_copy(
        src_ref=src,
        dst_ref=dst,
        send_sem=send_sem,
        recv_sem=recv_sem,
        device_id=target,
        device_id_type=MESH,
    )


def layer_kernel(
    head_ref, hidden_ref, gain_ref, routes_ref, weight_ref, proj_hbm, gate_hbm, up_hbm, down_hbm,
    mixed_ref,
    proj, gate, up, down, load_sem,
    heads, coeffs, rows, own, scaled, inverse, act,
    part32, part16, from_x, sum32, sum16, from_z,
    head_sem, coeff_z_sem, coeff_x_sem, rows_z_sem, rows_x_sem, x_sem, z_sem,
    hidden32, hidden16, hidden_in, hidden_sem, square_own, square_in, square_sem,
):
    sub = lax.axis_index("sub")
    dev = lax.axis_index("dev")
    z, x = dev // 2, dev % 2
    sibling, across = 1 - sub, z * 2 + (1 - x)
    width = rows.shape[2]
    half = head_ref.shape[0]

    loads = []
    for src, dst, parts in ((proj_hbm, proj, 1), (gate_hbm.at[0], gate, 4), (up_hbm.at[0], up, 4), (down_hbm.at[0], down, 4)):
        depth = dst.shape[0] // parts
        for p in range(parts):
            span = pl.ds(p * depth, depth)
            loads.append(pltpu.make_async_copy(src.at[span], dst.at[span], load_sem.at[len(loads)]))
    for load in loads:
        load.start()

    barrier = pltpu.get_barrier_semaphore()
    pl.semaphore_signal(barrier, inc=1, device_id={"sub": sibling}, device_id_type=MESH)
    pl.semaphore_signal(barrier, inc=1, device_id={"dev": across}, device_id_type=MESH)
    for dz in (1, 2, 3):
        pl.semaphore_signal(barrier, inc=1, device_id={"dev": (z + dz) % 4 * 2 + x}, device_id_type=MESH)
    pl.semaphore_wait(barrier, 5)

    def head_copy(who):
        return send(head_ref, heads.at[pl.ds(pl.multiple_of(who * half, half), half)], head_sem.at[0], head_sem.at[1], sub=sibling)

    head_copy(sub).start()
    heads[pl.ds(pl.multiple_of(sub * half, half), half), :] = head_ref[...]

    def block(buffer, owner):
        return buffer.at[pl.ds(pl.multiple_of(owner * ROWS, ROWS), ROWS)]

    def gather_z(buffer, sems, dz, owner_z):
        place = block(buffer, owner_z * 2 + x)
        return send(place, place, sems.at[0, dz - 1], sems.at[1, dz - 1], dev=(z + dz) % 4 * 2 + x)

    def gather_x(buffer, sems, dz, owner_x):
        place = block(buffer, (z - dz + 4) % 4 * 2 + owner_x)
        return send(place, place, sems.at[0, dz], sems.at[1, dz], dev=across)

    def gather_start(buffer, z_sems, x_sems):
        for dz in (2, 1, 3):
            gather_z(buffer, z_sems, dz, z).start()
        gather_x(buffer, x_sems, 0, x).start()

    def gather_forward(buffer, z_sems, x_sems):
        for dz in (1, 3, 2):
            gather_z(buffer, z_sems, dz, (z - dz + 4) % 4).wait_recv()
            gather_x(buffer, x_sems, dz, x).start()

    def gather_finish(buffer, z_sems, x_sems):
        for dz in (0, 1, 3, 2):
            gather_x(buffer, x_sems, dz, 1 - x).wait_recv()
            gather_x(buffer, x_sems, dz, x).wait_send()
        for dz in (1, 2, 3):
            gather_z(buffer, z_sems, dz, z).wait_send()

    lane = lax.broadcasted_iota(jnp.int32, (ROWS, 128), 1)
    table = jnp.zeros((ROWS, 128), jnp.float32)
    for j in range(routes_ref.shape[1]):
        table = table + jnp.where(lane == routes_ref[:, j : j + 1], weight_ref[:, j : j + 1], 0.0)
    coeffs[pl.ds(pl.multiple_of(dev * ROWS, ROWS), ROWS), :] = table
    gather_start(coeffs, coeff_z_sem, coeff_x_sem)

    def reduce_x(turn, c):
        return send(part16.at[turn, c, 1 - x], from_x.at[turn, c], x_sem.at[turn, 0, c], x_sem.at[turn, 1, c], dev=across)

    def reduce_z(turn, c, dz):
        there = (z + dz) % 4
        return send(sum16.at[turn, c, there], from_z.at[turn, c, dz - 1], z_sem.at[turn, 0, c, dz - 1], z_sem.at[turn, 1, c, dz - 1], dev=there * 2 + x)

    def reduce_start(turn, c, value):
        for d in range(2 * part32.shape[3]):
            piece = value[d * ROWS : (d + 1) * ROWS]
            part32[turn, c, d % 2, d // 2] = piece
            part16[turn, c, d % 2, d // 2] = piece.astype(jnp.bfloat16)
        reduce_x(turn, c).start()

    def reduce_forward(turn, c):
        reduce_x(turn, c).wait_recv()
        total = part32[turn, c, x] + from_x[turn, c].astype(jnp.float32)
        sum32[turn, c] = total
        sum16[turn, c] = total.astype(jnp.bfloat16)
        for dz in (2, 1, 3):
            reduce_z(turn, c, dz).start()

    def reduce_finish(turn, c):
        total = sum32[turn, c, z]
        for dz in (1, 3, 2):
            reduce_z(turn, c, dz).wait_recv()
            total = total + from_z[turn, c, dz - 1].astype(jnp.float32)
        return total

    def each(count, body):
        def step(i, carry):
            body(i)
            return carry

        lax.fori_loop(0, count, step, 0)

    def columns(c, size):
        return pl.ds(pl.multiple_of(c * size, size), size)

    loads[0].wait()
    head_copy(sibling).wait_recv()

    def project(c):
        reduce_start(0, c, jnp.dot(heads[...], proj[:, columns(c, width)], preferred_element_type=jnp.float32))

    each(PIECES, project)
    gather_forward(coeffs, coeff_z_sem, coeff_x_sem)
    each(PIECES, lambda c: reduce_forward(0, c))

    def settle(c):
        lanes = columns(c, width)
        residual = (hidden_ref[:, lanes].astype(jnp.float32) + reduce_finish(0, c)).astype(jnp.bfloat16)
        own[:, lanes] = residual
        rows[c, pl.ds(pl.multiple_of(dev * ROWS, ROWS), ROWS), :] = residual
        gather_start(rows.at[c], rows_z_sem.at[c], rows_x_sem.at[c])

    each(PIECES, settle)
    each(PIECES, lambda c: gather_forward(rows.at[c], rows_z_sem.at[c], rows_x_sem.at[c]))
    square_own[...] = jnp.zeros_like(square_own)

    def scale(c):
        gather_finish(rows.at[c], rows_z_sem.at[c], rows_x_sem.at[c])
        lanes = columns(c, width)
        value = rows[c].astype(jnp.float32)
        scaled[:, lanes] = (value * gain_ref[:, lanes]).astype(jnp.bfloat16)
        square_own[...] += jnp.broadcast_to(jnp.sum(value * value, axis=1, keepdims=True), square_own.shape)

    each(PIECES, scale)
    square_copy = send(square_own, square_in, square_sem.at[0], square_sem.at[1], sub=sibling)
    square_copy.start()
    for load in loads[1:9]:
        load.wait()

    def hidden_copy(t):
        return send(hidden16.at[t], hidden_in.at[t], hidden_sem.at[0, t], hidden_sem.at[1, t], sub=sibling)

    tiles = gate.shape[1] // TILE

    def enter(t):
        lanes = columns(t, TILE)
        for j, weights in enumerate((gate, up)):
            value = jnp.dot(scaled[...], weights[:, lanes], preferred_element_type=jnp.float32)
            hidden32[t, j] = value
            hidden16[t, j] = value.astype(jnp.bfloat16)
        hidden_copy(t).start()

    each(tiles, enter)
    square_copy.wait_recv()
    inverse[...] = lax.rsqrt((square_own[...] + square_in[...]) / D + EPS)
    gather_finish(coeffs, coeff_z_sem, coeff_x_sem)

    def activate(t):
        hidden_copy(t).wait_recv()
        factor = inverse[:, :1]
        opened = factor * (hidden32[t, 0] + hidden_in[t, 0].astype(jnp.float32))
        raised = factor * (hidden32[t, 1] + hidden_in[t, 1].astype(jnp.float32))
        act[:, columns(t, TILE)] = (opened / (1.0 + jnp.exp(-opened)) * raised).astype(jnp.bfloat16)

    each(tiles, activate)
    for load in loads[9:]:
        load.wait()

    def leave(c):
        mine = lax.broadcasted_iota(jnp.int32, coeffs.shape, 1) == z
        factor = jnp.sum(jnp.where(mine, coeffs[...], 0.0), axis=1, keepdims=True)
        produced = jnp.dot(act[...], down[:, columns(c, width)], preferred_element_type=jnp.float32)
        reduce_start(1, c, factor * produced)

    each(PIECES, leave)
    each(PIECES, lambda c: reduce_forward(1, c))

    def close(c):
        lanes = columns(c, width)
        mixed_ref[:, lanes] = (own[:, lanes].astype(jnp.float32) + reduce_finish(1, c)).astype(jnp.bfloat16)

    each(PIECES, close)
    head_copy(sub).wait_send()
    square_copy.wait_send()
    each(tiles, lambda t: hidden_copy(t).wait_send())

    def drain(c):
        for turn in range(2):
            reduce_x(turn, c).wait_send()
            for dz in (1, 2, 3):
                reduce_z(turn, c, dz).wait_send()

    each(PIECES, drain)


def run_layer(head_out, hidden, norm_gain, routes, route_weight, out_proj, expert_gate, expert_up, expert_down):
    depth, features = out_proj.shape
    inner = expert_gate.shape[2]
    reqs = 8 * ROWS
    width = features // PIECES
    tiles = inner // TILE
    vmem = pl.BlockSpec(memory_space=pltpu.VMEM)
    anywhere = pl.BlockSpec(memory_space=pl.ANY)
    bf16, f32, dma = jnp.bfloat16, jnp.float32, pltpu.SemaphoreType.DMA
    return pl.pallas_call(
        layer_kernel,
        in_specs=[vmem] * 5 + [anywhere] * 4,
        out_specs=vmem,
        out_shape=jax.ShapeDtypeStruct(hidden.shape, bf16),
        scratch_shapes=[
            pltpu.VMEM((depth, features), bf16),
            pltpu.VMEM((features, inner), bf16),
            pltpu.VMEM((features, inner), bf16),
            pltpu.VMEM((inner, features), bf16),
            dma((13,)),
            pltpu.VMEM((reqs, depth), bf16),
            pltpu.VMEM((reqs, 128), f32),
            pltpu.VMEM((PIECES, reqs, width), bf16),
            pltpu.VMEM((ROWS, features), bf16),
            pltpu.VMEM((reqs, features), bf16),
            pltpu.VMEM((reqs, 128), f32),
            pltpu.VMEM((reqs, inner), bf16),
            pltpu.VMEM((2, PIECES, 2, 4, ROWS, width), f32),
            pltpu.VMEM((2, PIECES, 2, 4, ROWS, width), bf16),
            pltpu.VMEM((2, PIECES, 4, ROWS, width), bf16),
            pltpu.VMEM((2, PIECES, 4, ROWS, width), f32),
            pltpu.VMEM((2, PIECES, 4, ROWS, width), bf16),
            pltpu.VMEM((2, PIECES, 3, ROWS, width), bf16),
            dma((2,)),
            dma((2, 3)),
            dma((2, 4)),
            dma((PIECES, 2, 3)),
            dma((PIECES, 2, 4)),
            dma((2, 2, PIECES)),
            dma((2, 2, PIECES, 3)),
            pltpu.VMEM((tiles, 2, reqs, TILE), f32),
            pltpu.VMEM((tiles, 2, reqs, TILE), bf16),
            pltpu.VMEM((tiles, 2, reqs, TILE), bf16),
            dma((2, tiles)),
            pltpu.VMEM((reqs, 128), f32),
            pltpu.VMEM((reqs, 128), f32),
            dma((2,)),
        ],
        compiler_params=pltpu.CompilerParams(
            collective_id=0, has_side_effects=True, vmem_limit_bytes=58 * 2**20
        ),
        name="layer",
    )(head_out, hidden, norm_gain.reshape(1, features), routes, route_weight, out_proj, expert_gate, expert_up, expert_down)


def fused_shards(
    hidden, new_query, new_key, new_value, out_gate, states, decay_rate, out_proj, norm_gain,
    routes, route_weight, expert_gate, expert_up, expert_down,
):
    new_states, head_out = update_states(new_query, new_key, new_value, out_gate, states, decay_rate)
    mixed = run_layer(head_out, hidden, norm_gain, routes, route_weight, out_proj, expert_gate, expert_up, expert_down)
    return (mixed, new_states)


def solution(mesh):
    sizes = dict(mesh.shape)
    fits = sizes["dev"] == 8 and sizes["tp"] == 1 and sizes["sub"] == 2
    placed = (
        P(("groups", "dev"), ("tp", "sub")),
        P(("groups", "tp", "sub"), "dev"),
        P(("groups", "tp", "sub"), "dev"),
        P(("groups", "tp", "sub"), "dev"),
        P(("groups", "tp", "sub"), "dev"),
        P(("groups", "tp", "sub"), "dev", None, None),
        P("dev"),
        P("dev", ("tp", "sub")),
        P(("tp", "sub")),
        P(("groups", "dev"), None),
        P(("groups", "dev"), None),
        P("dev", ("tp", "sub"), None),
        P("dev", ("tp", "sub"), None),
        P("dev", None, ("tp", "sub")),
    )
    return jax.shard_map(
        fused_shards if fits else shards,
        mesh=mesh,
        in_specs=placed,
        out_specs=(
            P(("groups", "dev"), ("tp", "sub")),
            P(("groups", "tp", "sub"), "dev", None, None),
        ),
        check_vma=False,
    )
```

```python
import jax
import jax.numpy as jnp
from jax import lax
from jax.experimental import pallas as pl
from jax.experimental.pallas import tpu as pltpu
from jax.sharding import PartitionSpec as P

D = 4096
SPLIT = 2


EPS = 1e-06


def route_tables(routes, route_weight, experts, slots):
    expert_ids = jnp.arange(experts, dtype=jnp.int32)
    chosen = routes[:, :, None] == expert_ids[None, None, :]
    member = jnp.any(chosen, axis=1).astype(jnp.int32)
    position = jnp.cumsum(member, axis=0) - member
    slot_ids = jnp.arange(slots, dtype=jnp.int32)
    placed = (member[:, :, None] == 1) & (position[:, :, None] == slot_ids[None, None, :])
    weights = jnp.sum(jnp.where(chosen, route_weight[:, :, None], jnp.float32(0.0)), axis=1)
    return (placed, weights)


def shards(
    hidden,
    new_query,
    new_key,
    new_value,
    out_gate,
    states,
    decay_rate,
    out_proj,
    norm_gain,
    routes,
    route_weight,
    expert_gate,
    expert_up,
    expert_down,
):
    local_reqs = states.shape[0]
    heads_here = states.shape[1]
    head_size = states.shape[3]
    query_heads = new_query.astype(jnp.float32).reshape(
        local_reqs, heads_here, head_size
    ) * head_size ** (-0.5)
    key_heads = new_key.astype(jnp.float32).reshape(local_reqs, heads_here, head_size)
    value_heads = new_value.astype(jnp.float32).reshape(local_reqs, heads_here, head_size)
    retain = jnp.exp(-decay_rate)
    updated = (
        retain[None, :, None, None] * states.astype(jnp.float32)
        + key_heads[:, :, :, None] * value_heads[:, :, None, :]
    )
    readout = jnp.einsum("rhi,rhij->rhj", query_heads, updated, precision=lax.Precision.HIGHEST)
    head_out = (
        jax.nn.sigmoid(out_gate.astype(jnp.float32))
        * readout.reshape(local_reqs, heads_here * head_size)
    ).astype(jnp.bfloat16)
    new_states = updated.astype(jnp.bfloat16)
    all_heads = lax.all_gather(head_out, ("tp", "sub"), axis=0, tiled=True)
    rows_here = hidden.shape[0]
    attended = lax.psum_scatter(
        jnp.dot(all_heads, out_proj, preferred_element_type=jnp.float32),
        "dev",
        scatter_dimension=0,
        tiled=True,
    )
    residual = (hidden.astype(jnp.float32) + attended).astype(jnp.bfloat16)
    feature_count = residual.shape[1]
    experts = lax.axis_size("dev") // SPLIT
    top_count = routes.shape[1]
    slots = min(rows_here, 2 * ((rows_here * top_count + experts - 1) // experts))
    placed, weights = route_tables(routes, route_weight, experts, slots)
    picks = placed.astype(jnp.bfloat16)
    outgoing = jnp.einsum(
        "nec,nd->ecd", picks, residual, preferred_element_type=jnp.float32
    ).astype(jnp.bfloat16)
    outgoing = jnp.repeat(outgoing, SPLIT, axis=0)
    received = lax.all_to_all(outgoing, "dev", split_axis=0, concat_axis=0, tiled=True)
    sources, count, width = received.shape
    flat_rows = received.reshape(sources * count, width).astype(jnp.float32)
    scaled = (flat_rows * norm_gain[None, :]).astype(jnp.bfloat16)
    gate_part = jnp.dot(scaled, expert_gate[0], preferred_element_type=jnp.float32)
    up_part = jnp.dot(scaled, expert_up[0], preferred_element_type=jnp.float32)
    squares = jnp.sum(flat_rows * flat_rows, axis=1)
    gate_sum, up_sum, square_sum = lax.psum((gate_part, up_part, squares), ("tp", "sub"))
    inverse = lax.rsqrt(square_sum / D + EPS)[:, None]
    act = (jax.nn.silu(inverse * gate_sum) * (inverse * up_sum)).astype(jnp.bfloat16)
    produced = jnp.dot(act, expert_down[0], preferred_element_type=jnp.float32)
    expert_out = produced.reshape(sources, count, width)
    returned = lax.all_to_all(expert_out, "dev", split_axis=0, concat_axis=0, tiled=True)
    merged = returned.reshape(experts, SPLIT, slots, feature_count).sum(axis=1)
    coeff = placed.astype(jnp.float32) * weights[:, :, None]
    mixture = jnp.einsum("nec,ecd->nd", coeff, merged, precision=lax.Precision.HIGHEST)
    mixed = (residual.astype(jnp.float32) + mixture).astype(jnp.bfloat16)
    return (mixed, new_states)


ROWS = 16
COPIES = 4
PIECES = 4
TILE = 256
MESH = pl.DeviceIdType.MESH


def state_kernel(q_ref, k_ref, v_ref, g_ref, d_ref, s_hbm, new_hbm, out_ref, old, new, in_sem, out_sem):
    reqs, heads, size = old.shape[0], old.shape[1], old.shape[3]
    steps = reqs // ROWS
    row_ids = lax.broadcasted_iota(jnp.int32, (ROWS, size), 0)
    part = ROWS // COPIES

    def span(i, p):
        return pl.ds(i * ROWS + p * part, part)

    def load(i, p):
        return pltpu.make_async_copy(s_hbm.at[span(i, p)], old.at[span(i, p)], in_sem.at[i, p])

    def store(i, p):
        return pltpu.make_async_copy(new.at[span(i, p)], new_hbm.at[span(i, p)], out_sem.at[i, p])

    for i in range(steps):
        for p in range(COPIES):
            load(i, p).start()

    def step(i, carry):
        here = pl.ds(pl.multiple_of(i * ROWS, ROWS), ROWS)
        for p in range(COPIES):
            load(i, p).wait()
        for h in range(heads):
            lanes = slice(h * size, (h + 1) * size)
            q = q_ref[here, lanes]
            q32 = q.astype(jnp.float32)
            k32 = k_ref[here, lanes].astype(jnp.float32)
            v32 = v_ref[here, lanes].astype(jnp.float32)
            columns = k32.T.astype(jnp.bfloat16)
            retain = jnp.exp(-d_ref[:, h : h + 1])
            read = jnp.zeros((ROWS, size), jnp.float32)
            for r in range(ROWS):
                state = old[i * ROWS + r, h]
                product = jnp.dot(q, state, preferred_element_type=jnp.float32)
                read = jnp.where(row_ids == r, product, read)
                only = jnp.where(row_ids == r, v32, 0.0).astype(jnp.bfloat16)
                outer = jnp.dot(columns, only, preferred_element_type=jnp.float32)
                new[i * ROWS + r, h] = (retain * state.astype(jnp.float32) + outer).astype(jnp.bfloat16)
            overlap = jnp.sum(q32 * k32, axis=1, keepdims=True)
            read = (retain * read + overlap * v32) * size ** (-0.5)
            gate = g_ref[here, lanes].astype(jnp.float32)
            out_ref[here, lanes] = (read / (1.0 + jnp.exp(-gate))).astype(jnp.bfloat16)
        for p in range(COPIES):
            store(i, p).start()
        return carry

    lax.fori_loop(0, steps, step, 0)
    for i in range(steps):
        for p in range(COPIES):
            store(i, p).wait()


def update_states(new_query, new_key, new_value, out_gate, states, decay_rate):
    reqs, heads, size = states.shape[0], states.shape[1], states.shape[3]
    vmem = pl.BlockSpec(memory_space=pltpu.VMEM)
    anywhere = pl.BlockSpec(memory_space=pl.ANY)
    sems = pltpu.SemaphoreType.DMA((reqs // ROWS, COPIES))
    return pl.pallas_call(
        state_kernel,
        in_specs=[vmem] * 5 + [anywhere],
        out_specs=[anywhere, vmem],
        out_shape=[
            jax.ShapeDtypeStruct(states.shape, jnp.bfloat16),
            jax.ShapeDtypeStruct((reqs, heads * size), jnp.bfloat16),
        ],
        scratch_shapes=[
            pltpu.VMEM(states.shape, jnp.bfloat16),
            pltpu.VMEM(states.shape, jnp.bfloat16),
            sems,
            sems,
        ],
        compiler_params=pltpu.CompilerParams(vmem_limit_bytes=60 * 2**20),
        name="states",
    )(new_query, new_key, new_value, out_gate, decay_rate.reshape(1, heads), states)


def send(src, dst, send_sem, recv_sem, **target):
    return pltpu.make_async_remote_copy(
        src_ref=src,
        dst_ref=dst,
        send_sem=send_sem,
        recv_sem=recv_sem,
        device_id=target,
        device_id_type=MESH,
    )


def layer_kernel(
    head_ref, hidden_ref, gain_ref, routes_ref, weight_ref, proj_hbm, gate_hbm, up_hbm, down_hbm,
    mixed_ref,
    proj, gate, up, down, load_sem,
    heads, coeffs, rows, own, scaled, inverse, act,
    part32, part16, from_x, sum32, sum16, from_z,
    head_sem, coeff_z_sem, coeff_x_sem, rows_z_sem, rows_x_sem, x_sem, z_sem,
    hidden32, hidden16, hidden_in, hidden_sem, square_own, square_in, square_sem,
):
    sub = lax.axis_index("sub")
    dev = lax.axis_index("dev")
    z, x = dev // 2, dev % 2
    sibling, across = 1 - sub, z * 2 + (1 - x)
    width = rows.shape[2]
    half = head_ref.shape[0]

    loads = []
    for src, dst, parts in ((proj_hbm, proj, 1), (gate_hbm.at[0], gate, 4), (up_hbm.at[0], up, 4), (down_hbm.at[0], down, 4)):
        depth = dst.shape[0] // parts
        for p in range(parts):
            span = pl.ds(p * depth, depth)
            loads.append(pltpu.make_async_copy(src.at[span], dst.at[span], load_sem.at[len(loads)]))
    for load in loads:
        load.start()

    barrier = pltpu.get_barrier_semaphore()
    pl.semaphore_signal(barrier, inc=1, device_id={"sub": sibling}, device_id_type=MESH)
    pl.semaphore_signal(barrier, inc=1, device_id={"dev": across}, device_id_type=MESH)
    for dz in (1, 2, 3):
        pl.semaphore_signal(barrier, inc=1, device_id={"dev": (z + dz) % 4 * 2 + x}, device_id_type=MESH)
    pl.semaphore_wait(barrier, 5)

    def head_copy(who):
        return send(head_ref, heads.at[pl.ds(pl.multiple_of(who * half, half), half)], head_sem.at[0], head_sem.at[1], sub=sibling)

    head_copy(sub).start()
    heads[pl.ds(pl.multiple_of(sub * half, half), half), :] = head_ref[...]

    def block(buffer, owner):
        return buffer.at[pl.ds(pl.multiple_of(owner * ROWS, ROWS), ROWS)]

    def gather_z(buffer, sems, dz, owner_z):
        place = block(buffer, owner_z * 2 + x)
        return send(place, place, sems.at[0, dz - 1], sems.at[1, dz - 1], dev=(z + dz) % 4 * 2 + x)

    def gather_x(buffer, sems, dz, owner_x):
        place = block(buffer, (z - dz + 4) % 4 * 2 + owner_x)
        return send(place, place, sems.at[0, dz], sems.at[1, dz], dev=across)

    def gather_start(buffer, z_sems, x_sems):
        for dz in (2, 1, 3):
            gather_z(buffer, z_sems, dz, z).start()
        gather_x(buffer, x_sems, 0, x).start()

    def gather_forward(buffer, z_sems, x_sems):
        for dz in (1, 3, 2):
            gather_z(buffer, z_sems, dz, (z - dz + 4) % 4).wait_recv()
            gather_x(buffer, x_sems, dz, x).start()

    def gather_finish(buffer, z_sems, x_sems):
        for dz in (0, 1, 3, 2):
            gather_x(buffer, x_sems, dz, 1 - x).wait_recv()
            gather_x(buffer, x_sems, dz, x).wait_send()
        for dz in (1, 2, 3):
            gather_z(buffer, z_sems, dz, z).wait_send()

    lane = lax.broadcasted_iota(jnp.int32, (ROWS, 128), 1)
    table = jnp.zeros((ROWS, 128), jnp.float32)
    square = (ROWS, ROWS)
    diagonal = lax.broadcasted_iota(jnp.int32, square, 0) == lax.broadcasted_iota(jnp.int32, square, 1)
    for j in range(routes_ref.shape[0]):
        chosen = jnp.broadcast_to(routes_ref[j : j + 1, :].astype(jnp.float32), square)
        chosen = jnp.sum(jnp.where(diagonal, chosen, 0.0), axis=1, keepdims=True)
        share = jnp.broadcast_to(weight_ref[j : j + 1, :], square)
        share = jnp.sum(jnp.where(diagonal, share, 0.0), axis=1, keepdims=True)
        table = table + jnp.where(lane == chosen.astype(jnp.int32), share, 0.0)
    coeffs[pl.ds(pl.multiple_of(dev * ROWS, ROWS), ROWS), :] = table
    gather_start(coeffs, coeff_z_sem, coeff_x_sem)

    def reduce_x(turn, c):
        return send(part16.at[turn, c, 1 - x], from_x.at[turn, c], x_sem.at[turn, 0, c], x_sem.at[turn, 1, c], dev=across)

    def reduce_z(turn, c, dz):
        there = (z + dz) % 4
        return send(sum16.at[turn, c, there], from_z.at[turn, c, dz - 1], z_sem.at[turn, 0, c, dz - 1], z_sem.at[turn, 1, c, dz - 1], dev=there * 2 + x)

    def reduce_start(turn, c, value):
        for d in range(2 * part32.shape[3]):
            piece = value[d * ROWS : (d + 1) * ROWS]
            part32[turn, c, d % 2, d // 2] = piece
            part16[turn, c, d % 2, d // 2] = piece.astype(jnp.bfloat16)
        reduce_x(turn, c).start()

    def reduce_forward(turn, c):
        reduce_x(turn, c).wait_recv()
        total = part32[turn, c, x] + from_x[turn, c].astype(jnp.float32)
        sum32[turn, c] = total
        sum16[turn, c] = total.astype(jnp.bfloat16)
        for dz in (2, 1, 3):
            reduce_z(turn, c, dz).start()

    def reduce_finish(turn, c):
        total = sum32[turn, c, z]
        for dz in (1, 3, 2):
            reduce_z(turn, c, dz).wait_recv()
            total = total + from_z[turn, c, dz - 1].astype(jnp.float32)
        return total

    def each(count, body):
        def step(i, carry):
            body(i)
            return carry

        lax.fori_loop(0, count, step, 0)

    def columns(c, size):
        return pl.ds(pl.multiple_of(c * size, size), size)

    loads[0].wait()
    head_copy(sibling).wait_recv()

    def project(c):
        reduce_start(0, c, jnp.dot(heads[...], proj[:, columns(c, width)], preferred_element_type=jnp.float32))

    each(PIECES, project)
    gather_forward(coeffs, coeff_z_sem, coeff_x_sem)
    each(PIECES, lambda c: reduce_forward(0, c))

    def settle(c):
        lanes = columns(c, width)
        residual = (hidden_ref[:, lanes].astype(jnp.float32) + reduce_finish(0, c)).astype(jnp.bfloat16)
        own[:, lanes] = residual
        rows[c, pl.ds(pl.multiple_of(dev * ROWS, ROWS), ROWS), :] = residual
        gather_start(rows.at[c], rows_z_sem.at[c], rows_x_sem.at[c])

    each(PIECES, settle)
    each(PIECES, lambda c: gather_forward(rows.at[c], rows_z_sem.at[c], rows_x_sem.at[c]))
    square_own[...] = jnp.zeros_like(square_own)

    def scale(c):
        gather_finish(rows.at[c], rows_z_sem.at[c], rows_x_sem.at[c])
        lanes = columns(c, width)
        value = rows[c].astype(jnp.float32)
        scaled[:, lanes] = (value * gain_ref[:, lanes]).astype(jnp.bfloat16)
        square_own[...] += jnp.broadcast_to(jnp.sum(value * value, axis=1, keepdims=True), square_own.shape)

    early = PIECES // 2
    split = early * width
    tiles = gate.shape[1] // TILE
    each(early, scale)
    for load in loads[1:9]:
        load.wait()

    def begin(t):
        lanes = columns(t, TILE)
        for j, weights in enumerate((gate, up)):
            hidden32[t, j] = jnp.dot(scaled[:, :split], weights[:split, lanes], preferred_element_type=jnp.float32)

    each(tiles, begin)
    each(PIECES - early, lambda c: scale(c + early))
    square_copy = send(square_own, square_in, square_sem.at[0], square_sem.at[1], sub=sibling)
    square_copy.start()

    def hidden_copy(t):
        return send(hidden16.at[t], hidden_in.at[t], hidden_sem.at[0, t], hidden_sem.at[1, t], sub=sibling)

    def enter(t):
        lanes = columns(t, TILE)
        for j, weights in enumerate((gate, up)):
            value = hidden32[t, j] + jnp.dot(scaled[:, split:], weights[split:, lanes], preferred_element_type=jnp.float32)
            hidden32[t, j] = value
            hidden16[t, j] = value.astype(jnp.bfloat16)
        hidden_copy(t).start()

    each(tiles, enter)
    square_copy.wait_recv()
    inverse[...] = lax.rsqrt((square_own[...] + square_in[...]) / D + EPS)
    gather_finish(coeffs, coeff_z_sem, coeff_x_sem)

    def activate(t):
        hidden_copy(t).wait_recv()
        factor = inverse[:, :1]
        opened = factor * (hidden32[t, 0] + hidden_in[t, 0].astype(jnp.float32))
        raised = factor * (hidden32[t, 1] + hidden_in[t, 1].astype(jnp.float32))
        act[:, columns(t, TILE)] = (opened / (1.0 + jnp.exp(-opened)) * raised).astype(jnp.bfloat16)

    each(tiles, activate)
    for load in loads[9:]:
        load.wait()

    def leave(c):
        mine = lax.broadcasted_iota(jnp.int32, coeffs.shape, 1) == z
        factor = jnp.sum(jnp.where(mine, coeffs[...], 0.0), axis=1, keepdims=True)
        produced = jnp.dot(act[...], down[:, columns(c, width)], preferred_element_type=jnp.float32)
        reduce_start(1, c, factor * produced)

    each(PIECES, leave)
    each(PIECES, lambda c: reduce_forward(1, c))

    def close(c):
        lanes = columns(c, width)
        mixed_ref[:, lanes] = (own[:, lanes].astype(jnp.float32) + reduce_finish(1, c)).astype(jnp.bfloat16)

    each(PIECES, close)
    head_copy(sub).wait_send()
    square_copy.wait_send()
    each(tiles, lambda t: hidden_copy(t).wait_send())

    def drain(c):
        for turn in range(2):
            reduce_x(turn, c).wait_send()
            for dz in (1, 2, 3):
                reduce_z(turn, c, dz).wait_send()

    each(PIECES, drain)


def run_layer(head_out, hidden, norm_gain, routes, route_weight, out_proj, expert_gate, expert_up, expert_down):
    depth, features = out_proj.shape
    inner = expert_gate.shape[2]
    reqs = 8 * ROWS
    width = features // PIECES
    tiles = inner // TILE
    vmem = pl.BlockSpec(memory_space=pltpu.VMEM)
    anywhere = pl.BlockSpec(memory_space=pl.ANY)
    bf16, f32, dma = jnp.bfloat16, jnp.float32, pltpu.SemaphoreType.DMA
    return pl.pallas_call(
        layer_kernel,
        in_specs=[vmem] * 5 + [anywhere] * 4,
        out_specs=vmem,
        out_shape=jax.ShapeDtypeStruct(hidden.shape, bf16),
        scratch_shapes=[
            pltpu.VMEM((depth, features), bf16),
            pltpu.VMEM((features, inner), bf16),
            pltpu.VMEM((features, inner), bf16),
            pltpu.VMEM((inner, features), bf16),
            dma((13,)),
            pltpu.VMEM((reqs, depth), bf16),
            pltpu.VMEM((reqs, 128), f32),
            pltpu.VMEM((PIECES, reqs, width), bf16),
            pltpu.VMEM((ROWS, features), bf16),
            pltpu.VMEM((reqs, features), bf16),
            pltpu.VMEM((reqs, 128), f32),
            pltpu.VMEM((reqs, inner), bf16),
            pltpu.VMEM((2, PIECES, 2, 4, ROWS, width), f32),
            pltpu.VMEM((2, PIECES, 2, 4, ROWS, width), bf16),
            pltpu.VMEM((2, PIECES, 4, ROWS, width), bf16),
            pltpu.VMEM((2, PIECES, 4, ROWS, width), f32),
            pltpu.VMEM((2, PIECES, 4, ROWS, width), bf16),
            pltpu.VMEM((2, PIECES, 3, ROWS, width), bf16),
            dma((2,)),
            dma((2, 3)),
            dma((2, 4)),
            dma((PIECES, 2, 3)),
            dma((PIECES, 2, 4)),
            dma((2, 2, PIECES)),
            dma((2, 2, PIECES, 3)),
            pltpu.VMEM((tiles, 2, reqs, TILE), f32),
            pltpu.VMEM((tiles, 2, reqs, TILE), bf16),
            pltpu.VMEM((tiles, 2, reqs, TILE), bf16),
            dma((2, tiles)),
            pltpu.VMEM((reqs, 128), f32),
            pltpu.VMEM((reqs, 128), f32),
            dma((2,)),
        ],
        compiler_params=pltpu.CompilerParams(
            collective_id=0, has_side_effects=True, vmem_limit_bytes=58 * 2**20
        ),
        name="layer",
    )(head_out, hidden, norm_gain.reshape(1, features), routes.T, route_weight.T, out_proj, expert_gate, expert_up, expert_down)


def fused_shards(
    hidden, new_query, new_key, new_value, out_gate, states, decay_rate, out_proj, norm_gain,
    routes, route_weight, expert_gate, expert_up, expert_down,
):
    new_states, head_out = update_states(new_query, new_key, new_value, out_gate, states, decay_rate)
    mixed = run_layer(head_out, hidden, norm_gain, routes, route_weight, out_proj, expert_gate, expert_up, expert_down)
    return (mixed, new_states)


def solution(mesh):
    sizes = dict(mesh.shape)
    fits = sizes["dev"] == 8 and sizes["tp"] == 1 and sizes["sub"] == 2
    placed = (
        P(("groups", "dev"), ("tp", "sub")),
        P(("groups", "tp", "sub"), "dev"),
        P(("groups", "tp", "sub"), "dev"),
        P(("groups", "tp", "sub"), "dev"),
        P(("groups", "tp", "sub"), "dev"),
        P(("groups", "tp", "sub"), "dev", None, None),
        P("dev"),
        P("dev", ("tp", "sub")),
        P(("tp", "sub")),
        P(("groups", "dev"), None),
        P(("groups", "dev"), None),
        P("dev", ("tp", "sub"), None),
        P("dev", ("tp", "sub"), None),
        P("dev", None, ("tp", "sub")),
    )
    return jax.shard_map(
        fused_shards if fits else shards,
        mesh=mesh,
        in_specs=placed,
        out_specs=(
            P(("groups", "dev"), ("tp", "sub")),
            P(("groups", "tp", "sub"), "dev", None, None),
        ),
        check_vma=False,
    )
```

```python
import jax
import jax.numpy as jnp
from jax import lax
from jax.experimental import pallas as pl
from jax.experimental.pallas import tpu as pltpu
from jax.sharding import PartitionSpec as P

D = 4096
SPLIT = 2


EPS = 1e-06


def route_tables(routes, route_weight, experts, slots):
    expert_ids = jnp.arange(experts, dtype=jnp.int32)
    chosen = routes[:, :, None] == expert_ids[None, None, :]
    member = jnp.any(chosen, axis=1).astype(jnp.int32)
    position = jnp.cumsum(member, axis=0) - member
    slot_ids = jnp.arange(slots, dtype=jnp.int32)
    placed = (member[:, :, None] == 1) & (position[:, :, None] == slot_ids[None, None, :])
    weights = jnp.sum(jnp.where(chosen, route_weight[:, :, None], jnp.float32(0.0)), axis=1)
    return (placed, weights)


def shards(
    hidden,
    new_query,
    new_key,
    new_value,
    out_gate,
    states,
    decay_rate,
    out_proj,
    norm_gain,
    routes,
    route_weight,
    expert_gate,
    expert_up,
    expert_down,
):
    local_reqs = states.shape[0]
    heads_here = states.shape[1]
    head_size = states.shape[3]
    query_heads = new_query.astype(jnp.float32).reshape(
        local_reqs, heads_here, head_size
    ) * head_size ** (-0.5)
    key_heads = new_key.astype(jnp.float32).reshape(local_reqs, heads_here, head_size)
    value_heads = new_value.astype(jnp.float32).reshape(local_reqs, heads_here, head_size)
    retain = jnp.exp(-decay_rate)
    updated = (
        retain[None, :, None, None] * states.astype(jnp.float32)
        + key_heads[:, :, :, None] * value_heads[:, :, None, :]
    )
    readout = jnp.einsum("rhi,rhij->rhj", query_heads, updated, precision=lax.Precision.HIGHEST)
    head_out = (
        jax.nn.sigmoid(out_gate.astype(jnp.float32))
        * readout.reshape(local_reqs, heads_here * head_size)
    ).astype(jnp.bfloat16)
    new_states = updated.astype(jnp.bfloat16)
    all_heads = lax.all_gather(head_out, ("tp", "sub"), axis=0, tiled=True)
    rows_here = hidden.shape[0]
    attended = lax.psum_scatter(
        jnp.dot(all_heads, out_proj, preferred_element_type=jnp.float32),
        "dev",
        scatter_dimension=0,
        tiled=True,
    )
    residual = (hidden.astype(jnp.float32) + attended).astype(jnp.bfloat16)
    feature_count = residual.shape[1]
    experts = lax.axis_size("dev") // SPLIT
    top_count = routes.shape[1]
    slots = min(rows_here, 2 * ((rows_here * top_count + experts - 1) // experts))
    placed, weights = route_tables(routes, route_weight, experts, slots)
    picks = placed.astype(jnp.bfloat16)
    outgoing = jnp.einsum(
        "nec,nd->ecd", picks, residual, preferred_element_type=jnp.float32
    ).astype(jnp.bfloat16)
    outgoing = jnp.repeat(outgoing, SPLIT, axis=0)
    received = lax.all_to_all(outgoing, "dev", split_axis=0, concat_axis=0, tiled=True)
    sources, count, width = received.shape
    flat_rows = received.reshape(sources * count, width).astype(jnp.float32)
    scaled = (flat_rows * norm_gain[None, :]).astype(jnp.bfloat16)
    gate_part = jnp.dot(scaled, expert_gate[0], preferred_element_type=jnp.float32)
    up_part = jnp.dot(scaled, expert_up[0], preferred_element_type=jnp.float32)
    squares = jnp.sum(flat_rows * flat_rows, axis=1)
    gate_sum, up_sum, square_sum = lax.psum((gate_part, up_part, squares), ("tp", "sub"))
    inverse = lax.rsqrt(square_sum / D + EPS)[:, None]
    act = (jax.nn.silu(inverse * gate_sum) * (inverse * up_sum)).astype(jnp.bfloat16)
    produced = jnp.dot(act, expert_down[0], preferred_element_type=jnp.float32)
    expert_out = produced.reshape(sources, count, width)
    returned = lax.all_to_all(expert_out, "dev", split_axis=0, concat_axis=0, tiled=True)
    merged = returned.reshape(experts, SPLIT, slots, feature_count).sum(axis=1)
    coeff = placed.astype(jnp.float32) * weights[:, :, None]
    mixture = jnp.einsum("nec,ecd->nd", coeff, merged, precision=lax.Precision.HIGHEST)
    mixed = (residual.astype(jnp.float32) + mixture).astype(jnp.bfloat16)
    return (mixed, new_states)


ROWS = 16
COPIES = 4
PIECES = 4
TILE = 256
MESH = pl.DeviceIdType.MESH


def state_kernel(q_ref, k_ref, v_ref, g_ref, d_ref, s_hbm, new_hbm, out_ref, old, new, in_sem, out_sem):
    reqs, heads, size = old.shape[0], old.shape[1], old.shape[3]
    steps = reqs // ROWS
    row_ids = lax.broadcasted_iota(jnp.int32, (ROWS, size), 0)
    part = ROWS // COPIES

    def span(i, p):
        return pl.ds(i * ROWS + p * part, part)

    def load(i, p):
        return pltpu.make_async_copy(s_hbm.at[span(i, p)], old.at[span(i, p)], in_sem.at[i, p])

    def store(i, p):
        return pltpu.make_async_copy(new.at[span(i, p)], new_hbm.at[span(i, p)], out_sem.at[i, p])

    for i in range(steps):
        for p in range(COPIES):
            load(i, p).start()

    def step(i, carry):
        here = pl.ds(pl.multiple_of(i * ROWS, ROWS), ROWS)
        for p in range(COPIES):
            load(i, p).wait()
        for h in range(heads):
            lanes = slice(h * size, (h + 1) * size)
            q = q_ref[here, lanes]
            q32 = q.astype(jnp.float32)
            k32 = k_ref[here, lanes].astype(jnp.float32)
            v32 = v_ref[here, lanes].astype(jnp.float32)
            columns = k32.T.astype(jnp.bfloat16)
            retain = jnp.exp(-d_ref[:, h : h + 1])
            read = jnp.zeros((ROWS, size), jnp.float32)
            for r in range(ROWS):
                state = old[i * ROWS + r, h]
                product = jnp.dot(q, state, preferred_element_type=jnp.float32)
                read = jnp.where(row_ids == r, product, read)
                only = jnp.where(row_ids == r, v32, 0.0).astype(jnp.bfloat16)
                outer = jnp.dot(columns, only, preferred_element_type=jnp.float32)
                new[i * ROWS + r, h] = (retain * state.astype(jnp.float32) + outer).astype(jnp.bfloat16)
            overlap = jnp.sum(q32 * k32, axis=1, keepdims=True)
            read = (retain * read + overlap * v32) * size ** (-0.5)
            gate = g_ref[here, lanes].astype(jnp.float32)
            out_ref[here, lanes] = (read / (1.0 + jnp.exp(-gate))).astype(jnp.bfloat16)
        for p in range(COPIES):
            store(i, p).start()
        return carry

    lax.fori_loop(0, steps, step, 0)
    for i in range(steps):
        for p in range(COPIES):
            store(i, p).wait()


def update_states(new_query, new_key, new_value, out_gate, states, decay_rate):
    reqs, heads, size = states.shape[0], states.shape[1], states.shape[3]
    vmem = pl.BlockSpec(memory_space=pltpu.VMEM)
    anywhere = pl.BlockSpec(memory_space=pl.ANY)
    sems = pltpu.SemaphoreType.DMA((reqs // ROWS, COPIES))
    return pl.pallas_call(
        state_kernel,
        in_specs=[vmem] * 5 + [anywhere],
        out_specs=[anywhere, vmem],
        out_shape=[
            jax.ShapeDtypeStruct(states.shape, jnp.bfloat16),
            jax.ShapeDtypeStruct((reqs, heads * size), jnp.bfloat16),
        ],
        scratch_shapes=[
            pltpu.VMEM(states.shape, jnp.bfloat16),
            pltpu.VMEM(states.shape, jnp.bfloat16),
            sems,
            sems,
        ],
        compiler_params=pltpu.CompilerParams(vmem_limit_bytes=60 * 2**20),
        name="states",
    )(new_query, new_key, new_value, out_gate, decay_rate.reshape(1, heads), states)


def send(src, dst, send_sem, recv_sem, **target):
    return pltpu.make_async_remote_copy(
        src_ref=src,
        dst_ref=dst,
        send_sem=send_sem,
        recv_sem=recv_sem,
        device_id=target,
        device_id_type=MESH,
    )


def layer_kernel(
    head_ref, hidden_ref, gain_ref, routes_ref, weight_ref, proj_hbm, gate_hbm, up_hbm, down_hbm,
    mixed_ref,
    proj, gate, up, down, load_sem,
    heads, coeffs, rows, own, scaled, inverse, act,
    part32, part16, from_x, sum32, sum16, from_z,
    head_sem, coeff_z_sem, coeff_x_sem, rows_z_sem, rows_x_sem, x_sem, z_sem,
    hidden32, hidden16, hidden_in, hidden_sem, square_own, square_in, square_sem,
):
    sub = lax.axis_index("sub")
    dev = lax.axis_index("dev")
    z, x = dev // 2, dev % 2
    sibling, across = 1 - sub, z * 2 + (1 - x)
    width = rows.shape[2]
    half = head_ref.shape[0]

    loads = []
    for src, dst, parts in ((proj_hbm, proj, 1), (gate_hbm.at[0], gate, 4), (up_hbm.at[0], up, 4), (down_hbm.at[0], down, 4)):
        depth = dst.shape[0] // parts
        for p in range(parts):
            span = pl.ds(p * depth, depth)
            loads.append(pltpu.make_async_copy(src.at[span], dst.at[span], load_sem.at[len(loads)]))
    loads[0].start()

    barrier = pltpu.get_barrier_semaphore()
    pl.semaphore_signal(barrier, inc=1, device_id={"sub": sibling}, device_id_type=MESH)
    pl.semaphore_signal(barrier, inc=1, device_id={"dev": across}, device_id_type=MESH)
    for dz in (1, 2, 3):
        pl.semaphore_signal(barrier, inc=1, device_id={"dev": (z + dz) % 4 * 2 + x}, device_id_type=MESH)
    pl.semaphore_wait(barrier, 5)

    def head_copy(who):
        return send(head_ref, heads.at[pl.ds(pl.multiple_of(who * half, half), half)], head_sem.at[0], head_sem.at[1], sub=sibling)

    head_copy(sub).start()
    heads[pl.ds(pl.multiple_of(sub * half, half), half), :] = head_ref[...]

    def block(buffer, owner):
        return buffer.at[pl.ds(pl.multiple_of(owner * ROWS, ROWS), ROWS)]

    def gather_z(buffer, sems, dz, owner_z):
        place = block(buffer, owner_z * 2 + x)
        return send(place, place, sems.at[0, dz - 1], sems.at[1, dz - 1], dev=(z + dz) % 4 * 2 + x)

    def gather_x(buffer, sems, dz, owner_x):
        place = block(buffer, (z - dz + 4) % 4 * 2 + owner_x)
        return send(place, place, sems.at[0, dz], sems.at[1, dz], dev=across)

    def gather_start(buffer, z_sems, x_sems):
        for dz in (2, 1, 3):
            gather_z(buffer, z_sems, dz, z).start()
        gather_x(buffer, x_sems, 0, x).start()

    def gather_forward(buffer, z_sems, x_sems):
        for dz in (1, 3, 2):
            gather_z(buffer, z_sems, dz, (z - dz + 4) % 4).wait_recv()
            gather_x(buffer, x_sems, dz, x).start()

    def gather_finish(buffer, z_sems, x_sems):
        for dz in (0, 1, 3, 2):
            gather_x(buffer, x_sems, dz, 1 - x).wait_recv()
            gather_x(buffer, x_sems, dz, x).wait_send()
        for dz in (1, 2, 3):
            gather_z(buffer, z_sems, dz, z).wait_send()

    lane = lax.broadcasted_iota(jnp.int32, (ROWS, 128), 1)
    table = jnp.zeros((ROWS, 128), jnp.float32)
    square = (ROWS, ROWS)
    diagonal = lax.broadcasted_iota(jnp.int32, square, 0) == lax.broadcasted_iota(jnp.int32, square, 1)
    for j in range(routes_ref.shape[0]):
        chosen = jnp.broadcast_to(routes_ref[j : j + 1, :].astype(jnp.float32), square)
        chosen = jnp.sum(jnp.where(diagonal, chosen, 0.0), axis=1, keepdims=True)
        share = jnp.broadcast_to(weight_ref[j : j + 1, :], square)
        share = jnp.sum(jnp.where(diagonal, share, 0.0), axis=1, keepdims=True)
        table = table + jnp.where(lane == chosen.astype(jnp.int32), share, 0.0)
    coeffs[pl.ds(pl.multiple_of(dev * ROWS, ROWS), ROWS), :] = table
    gather_start(coeffs, coeff_z_sem, coeff_x_sem)

    def reduce_x(turn, c):
        return send(part16.at[turn, c, 1 - x], from_x.at[turn, c], x_sem.at[turn, 0, c], x_sem.at[turn, 1, c], dev=across)

    def reduce_z(turn, c, dz):
        there = (z + dz) % 4
        return send(sum16.at[turn, c, there], from_z.at[turn, c, dz - 1], z_sem.at[turn, 0, c, dz - 1], z_sem.at[turn, 1, c, dz - 1], dev=there * 2 + x)

    def reduce_start(turn, c, value):
        for d in range(2 * part32.shape[3]):
            piece = value[d * ROWS : (d + 1) * ROWS]
            part32[turn, c, d % 2, d // 2] = piece
            part16[turn, c, d % 2, d // 2] = piece.astype(jnp.bfloat16)
        reduce_x(turn, c).start()

    def reduce_forward(turn, c):
        reduce_x(turn, c).wait_recv()
        total = part32[turn, c, x] + from_x[turn, c].astype(jnp.float32)
        sum32[turn, c] = total
        sum16[turn, c] = total.astype(jnp.bfloat16)
        for dz in (2, 1, 3):
            reduce_z(turn, c, dz).start()

    def reduce_finish(turn, c):
        total = sum32[turn, c, z]
        for dz in (1, 3, 2):
            reduce_z(turn, c, dz).wait_recv()
            total = total + from_z[turn, c, dz - 1].astype(jnp.float32)
        return total

    def each(count, body):
        def step(i, carry):
            body(i)
            return carry

        lax.fori_loop(0, count, step, 0)

    def columns(c, size):
        return pl.ds(pl.multiple_of(c * size, size), size)

    loads[0].wait()
    head_copy(sibling).wait_recv()

    def project(c):
        reduce_start(0, c, jnp.dot(heads[...], proj[:, columns(c, width)], preferred_element_type=jnp.float32))

    each(PIECES, project)
    for load in loads[1:5]:
        load.start()
    gather_forward(coeffs, coeff_z_sem, coeff_x_sem)
    each(PIECES, lambda c: reduce_forward(0, c))
    for load in loads[5:9]:
        load.start()

    def settle(c):
        lanes = columns(c, width)
        residual = (hidden_ref[:, lanes].astype(jnp.float32) + reduce_finish(0, c)).astype(jnp.bfloat16)
        own[:, lanes] = residual
        rows[c, pl.ds(pl.multiple_of(dev * ROWS, ROWS), ROWS), :] = residual
        gather_start(rows.at[c], rows_z_sem.at[c], rows_x_sem.at[c])

    each(PIECES, settle)
    each(PIECES, lambda c: gather_forward(rows.at[c], rows_z_sem.at[c], rows_x_sem.at[c]))
    for load in loads[9:]:
        load.start()
    square_own[...] = jnp.zeros_like(square_own)

    def scale(c):
        gather_finish(rows.at[c], rows_z_sem.at[c], rows_x_sem.at[c])
        lanes = columns(c, width)
        value = rows[c].astype(jnp.float32)
        scaled[:, lanes] = (value * gain_ref[:, lanes]).astype(jnp.bfloat16)
        square_own[...] += jnp.broadcast_to(jnp.sum(value * value, axis=1, keepdims=True), square_own.shape)

    early = PIECES // 2
    split = early * width
    tiles = gate.shape[1] // TILE
    each(early, scale)
    for load in loads[1:9]:
        load.wait()

    def begin(t):
        lanes = columns(t, TILE)
        for j, weights in enumerate((gate, up)):
            hidden32[t, j] = jnp.dot(scaled[:, :split], weights[:split, lanes], preferred_element_type=jnp.float32)

    each(tiles, begin)
    each(PIECES - early, lambda c: scale(c + early))
    square_copy = send(square_own, square_in, square_sem.at[0], square_sem.at[1], sub=sibling)
    square_copy.start()

    def hidden_copy(t):
        return send(hidden16.at[t], hidden_in.at[t], hidden_sem.at[0, t], hidden_sem.at[1, t], sub=sibling)

    def enter(t):
        lanes = columns(t, TILE)
        for j, weights in enumerate((gate, up)):
            value = hidden32[t, j] + jnp.dot(scaled[:, split:], weights[split:, lanes], preferred_element_type=jnp.float32)
            hidden32[t, j] = value
            hidden16[t, j] = value.astype(jnp.bfloat16)
        hidden_copy(t).start()

    each(tiles, enter)
    square_copy.wait_recv()
    inverse[...] = lax.rsqrt((square_own[...] + square_in[...]) / D + EPS)
    gather_finish(coeffs, coeff_z_sem, coeff_x_sem)

    def activate(t):
        hidden_copy(t).wait_recv()
        factor = inverse[:, :1]
        opened = factor * (hidden32[t, 0] + hidden_in[t, 0].astype(jnp.float32))
        raised = factor * (hidden32[t, 1] + hidden_in[t, 1].astype(jnp.float32))
        act[:, columns(t, TILE)] = (opened / (1.0 + jnp.exp(-opened)) * raised).astype(jnp.bfloat16)

    each(tiles, activate)
    for load in loads[9:]:
        load.wait()

    def leave(c):
        mine = lax.broadcasted_iota(jnp.int32, coeffs.shape, 1) == z
        factor = jnp.sum(jnp.where(mine, coeffs[...], 0.0), axis=1, keepdims=True)
        produced = jnp.dot(act[...], down[:, columns(c, width)], preferred_element_type=jnp.float32)
        reduce_start(1, c, factor * produced)

    each(PIECES, leave)
    each(PIECES, lambda c: reduce_forward(1, c))

    def close(c):
        lanes = columns(c, width)
        mixed_ref[:, lanes] = (own[:, lanes].astype(jnp.float32) + reduce_finish(1, c)).astype(jnp.bfloat16)

    each(PIECES, close)
    head_copy(sub).wait_send()
    square_copy.wait_send()
    each(tiles, lambda t: hidden_copy(t).wait_send())

    def drain(c):
        for turn in range(2):
            reduce_x(turn, c).wait_send()
            for dz in (1, 2, 3):
                reduce_z(turn, c, dz).wait_send()

    each(PIECES, drain)


def run_layer(head_out, hidden, norm_gain, routes, route_weight, out_proj, expert_gate, expert_up, expert_down):
    depth, features = out_proj.shape
    inner = expert_gate.shape[2]
    reqs = 8 * ROWS
    width = features // PIECES
    tiles = inner // TILE
    vmem = pl.BlockSpec(memory_space=pltpu.VMEM)
    anywhere = pl.BlockSpec(memory_space=pl.ANY)
    bf16, f32, dma = jnp.bfloat16, jnp.float32, pltpu.SemaphoreType.DMA
    return pl.pallas_call(
        layer_kernel,
        in_specs=[vmem] * 5 + [anywhere] * 4,
        out_specs=vmem,
        out_shape=jax.ShapeDtypeStruct(hidden.shape, bf16),
        scratch_shapes=[
            pltpu.VMEM((depth, features), bf16),
            pltpu.VMEM((features, inner), bf16),
            pltpu.VMEM((features, inner), bf16),
            pltpu.VMEM((inner, features), bf16),
            dma((13,)),
            pltpu.VMEM((reqs, depth), bf16),
            pltpu.VMEM((reqs, 128), f32),
            pltpu.VMEM((PIECES, reqs, width), bf16),
            pltpu.VMEM((ROWS, features), bf16),
            pltpu.VMEM((reqs, features), bf16),
            pltpu.VMEM((reqs, 128), f32),
            pltpu.VMEM((reqs, inner), bf16),
            pltpu.VMEM((2, PIECES, 2, 4, ROWS, width), f32),
            pltpu.VMEM((2, PIECES, 2, 4, ROWS, width), bf16),
            pltpu.VMEM((2, PIECES, 4, ROWS, width), bf16),
            pltpu.VMEM((2, PIECES, 4, ROWS, width), f32),
            pltpu.VMEM((2, PIECES, 4, ROWS, width), bf16),
            pltpu.VMEM((2, PIECES, 3, ROWS, width), bf16),
            dma((2,)),
            dma((2, 3)),
            dma((2, 4)),
            dma((PIECES, 2, 3)),
            dma((PIECES, 2, 4)),
            dma((2, 2, PIECES)),
            dma((2, 2, PIECES, 3)),
            pltpu.VMEM((tiles, 2, reqs, TILE), f32),
            pltpu.VMEM((tiles, 2, reqs, TILE), bf16),
            pltpu.VMEM((tiles, 2, reqs, TILE), bf16),
            dma((2, tiles)),
            pltpu.VMEM((reqs, 128), f32),
            pltpu.VMEM((reqs, 128), f32),
            dma((2,)),
        ],
        compiler_params=pltpu.CompilerParams(
            collective_id=0, has_side_effects=True, vmem_limit_bytes=58 * 2**20
        ),
        name="layer",
    )(head_out, hidden, norm_gain.reshape(1, features), routes.T, route_weight.T, out_proj, expert_gate, expert_up, expert_down)


def fused_shards(
    hidden, new_query, new_key, new_value, out_gate, states, decay_rate, out_proj, norm_gain,
    routes, route_weight, expert_gate, expert_up, expert_down,
):
    new_states, head_out = update_states(new_query, new_key, new_value, out_gate, states, decay_rate)
    mixed = run_layer(head_out, hidden, norm_gain, routes, route_weight, out_proj, expert_gate, expert_up, expert_down)
    return (mixed, new_states)


def solution(mesh):
    sizes = dict(mesh.shape)
    fits = sizes["dev"] == 8 and sizes["tp"] == 1 and sizes["sub"] == 2
    placed = (
        P(("groups", "dev"), ("tp", "sub")),
        P(("groups", "tp", "sub"), "dev"),
        P(("groups", "tp", "sub"), "dev"),
        P(("groups", "tp", "sub"), "dev"),
        P(("groups", "tp", "sub"), "dev"),
        P(("groups", "tp", "sub"), "dev", None, None),
        P("dev"),
        P("dev", ("tp", "sub")),
        P(("tp", "sub")),
        P(("groups", "dev"), None),
        P(("groups", "dev"), None),
        P("dev", ("tp", "sub"), None),
        P("dev", ("tp", "sub"), None),
        P("dev", None, ("tp", "sub")),
    )
    return jax.shard_map(
        fused_shards if fits else shards,
        mesh=mesh,
        in_specs=placed,
        out_specs=(
            P(("groups", "dev"), ("tp", "sub")),
            P(("groups", "tp", "sub"), "dev", None, None),
        ),
        check_vma=False,
    )
```
